256 devices in a mesh: dp: 8 (over x, core), head: 32 (over z, y).
Axes of the slice: x: 4, y: 4, z: 8, core: 2. Of those that a mesh axis runs over, the one named last changes fastest.
Arguments:
- query_latent: bfloat16 [4, 256, 1536], P(None, ('dp', 'head')), may hold values from -6 to 6
- query_weight: bfloat16 [1536, 24576], P(('dp', 'head')), may hold values from -0.15625 to 0.15625
- key_weight: bfloat16 [512, 16384], P(('dp', 'head')), may hold values from -0.25 to 0.25
- value_weight: bfloat16 [512, 16384], P(('dp', 'head')), may hold values from -0.25 to 0.25
- cache_latent: bfloat16 [256, 2048, 512], P(('dp', 'head')), may hold values from -6 to 6
- cache_rope: bfloat16 [256, 64, 2048], P(('dp', 'head')), may hold values from -1000 to 1000
- new_latent: bfloat16 [4, 256, 512], P(None, ('dp', 'head')), may hold values from -6 to 6
- new_rope: bfloat16 [4, 256, 64], P(None, ('dp', 'head')), may hold values from -6 to 6
- lengths: int32 [256], P(('dp', 'head')), may hold values from 1 to 2048, as said below
Outputs:
- attended: bfloat16 [4, 256, 16384], P(None, 'dp', 'head')
The draws below stay inside these ranges and needn't reach their ends.
Inputs may be any that keep to these rules, and one draw needn't show every extreme that they name: `lengths`: each sequence has at least one filled slot; some sequence fills all 2048.
All inputs are finite; a program needn't handle non-finite values.
Results may differ from the reference program's by a relative error of at most 0.014.
Values may be sent and summed in bfloat16 or wider, within the bound.
A program may use at most 128 MiB of HBM per device.

```python
import jax
import jax.numpy as jnp
from jax import lax

QR = 1536
KVR = 512
H = 128
DN = 128
DR = 64
DV = 128
CACHE = 2048
STEPS = 4
BATCH = 256


def draw_cache_rope(key, part):
    key = jax.random.fold_in(key, 11)
    first = jax.random.fold_in(key, 0)
    values = jax.random.normal(first, (BATCH, DR, CACHE), jnp.float32)
    return values.astype(jnp.bfloat16)


def draw_lengths(key, part):
    key = jax.random.fold_in(key, 12)
    first, second, third = jax.random.split(key, 3)
    upper = jax.random.randint(first, (BATCH,), 1, CACHE + 1)
    lower = jax.random.randint(second, (BATCH,), 1, CACHE + 1)
    filled = jnp.minimum(upper, lower)
    chosen = jax.random.randint(third, (), 0, BATCH)
    return filled.at[chosen].set(CACHE).astype(jnp.int32)


def block_levels(key, dims, cuts, least, top_value):
    def one(axis_at, parts):
        draws = jax.random.uniform(jax.random.fold_in(jax.random.fold_in(key, 6), axis_at), (parts,), jnp.float32, least / len(cuts), top_value / len(cuts))
        return jnp.repeat(jnp.exp(draws), dims[axis_at] // parts).reshape((-1,) + (1,) * (len(dims) - axis_at - 1))

    loudness = one(*cuts[0])
    for cut in cuts[1:]:
        loudness = loudness * one(*cut)
    return loudness


def scatter_about(key, extent, scale, most, shards=(), held_as=jnp.bfloat16):
    array = jax.random.normal(key, extent, jnp.float32) * scale
    if len(shards) > 0:
        array = block_levels(key, extent, shards, -0.22, 0.18) * array
    return jnp.clip(array, min=-most, max=most).astype(held_as)


def setup_inputs(seed: int = 0) -> dict:
    seeds = jax.random.split(jax.random.key(seed), 10)
    return {
        "query_latent": scatter_about(seeds[0], (STEPS, BATCH, QR), 1.0, 6.0, ((1, 256),)),
        "query_weight": scatter_about(seeds[1], (QR, H * (DN + DR)), QR ** -0.5, 0.15625, ((0, 256),)),
        "key_weight": scatter_about(seeds[2], (KVR, H * DN), KVR ** -0.5, 0.25, ((0, 256),)),
        "value_weight": scatter_about(seeds[3], (KVR, H * DV), KVR ** -0.5, 0.25, ((0, 256),)),
        "cache_latent": scatter_about(seeds[4], (BATCH, CACHE, KVR), 1.0, 6.0, ((0, 256),)),
        "cache_rope": draw_cache_rope(jax.random.fold_in(seeds[9], 71), 0),
        "new_latent": scatter_about(seeds[6], (STEPS, BATCH, KVR), 1.0, 6.0, ((1, 256),)),
        "new_rope": scatter_about(seeds[7], (STEPS, BATCH, DR), 1.0, 6.0, ((1, 256),)),
        "lengths": draw_lengths(jax.random.fold_in(seeds[9], 71), 0),
    }


def attend(query_abs, query_pos, latent, rope, fresh_latent, fresh_rope, length):
    steps_here = query_abs.shape[0]
    heads = query_abs.shape[1]
    scale = (DN + DR) ** -0.5
    query_rows = query_abs.reshape(steps_here * heads, KVR)
    pos_rows = query_pos.reshape(steps_here * heads, DR)
    cached = (jnp.dot(query_rows, latent.T, preferred_element_type=jnp.float32)
              + jnp.dot(pos_rows, rope, preferred_element_type=jnp.float32)) * scale
    fresh = (jnp.dot(query_rows, fresh_latent.T, preferred_element_type=jnp.float32)
             + jnp.dot(pos_rows, fresh_rope.T, preferred_element_type=jnp.float32)) * scale
    slots = jnp.arange(latent.shape[0], dtype=jnp.int32)
    cached = jnp.where(slots[None, :] < length, cached, jnp.float32(-1e30))
    row_step = jnp.arange(steps_here * heads, dtype=jnp.int32) // heads
    later = jnp.arange(steps_here, dtype=jnp.int32)
    fresh = jnp.where(later[None, :] <= row_step[:, None], fresh, jnp.float32(-1e30))
    top = jnp.maximum(jnp.max(cached, axis=1, keepdims=True), jnp.max(fresh, axis=1, keepdims=True))
    exp_cached = jnp.exp(cached - top)
    exp_fresh = jnp.exp(fresh - top)
    total = jnp.sum(exp_cached, axis=1, keepdims=True) + jnp.sum(exp_fresh, axis=1, keepdims=True)
    probs_cached = (exp_cached / total).astype(jnp.bfloat16)
    probs_fresh = (exp_fresh / total).astype(jnp.bfloat16)
    mixed = (jnp.dot(probs_cached, latent, preferred_element_type=jnp.float32)
             + jnp.dot(probs_fresh, fresh_latent, preferred_element_type=jnp.float32))
    return mixed.astype(jnp.bfloat16).reshape(steps_here, heads, KVR)


def reference(query_latent, query_weight, key_weight, value_weight, cache_latent, cache_rope, new_latent, new_rope, lengths):
    weight_heads = query_weight.reshape(QR, H, DN + DR)
    key_heads = key_weight.reshape(KVR, H, DN)
    absorbed = jnp.einsum("chd,khd->hck", weight_heads[:, :, :DN].astype(jnp.float32),
                          key_heads.astype(jnp.float32)).astype(jnp.bfloat16)
    query_rows = query_latent.reshape(STEPS * BATCH, QR)
    query_abs = jnp.einsum("rc,hck->rhk", query_rows.astype(jnp.float32),
                           absorbed.astype(jnp.float32)).astype(jnp.bfloat16)
    query_abs = query_abs.reshape(STEPS, BATCH, H, KVR)
    pos_weight = weight_heads[:, :, DN:].reshape(QR, H * DR)
    query_pos = jnp.dot(query_rows, pos_weight, preferred_element_type=jnp.float32).astype(jnp.bfloat16)
    query_pos = query_pos.reshape(STEPS, BATCH, H, DR)

    def one_sequence(items):
        return attend(*items)

    latent_out = lax.map(one_sequence, (jnp.swapaxes(query_abs, 0, 1), jnp.swapaxes(query_pos, 0, 1),
                                        cache_latent, cache_rope, jnp.swapaxes(new_latent, 0, 1),
                                        jnp.swapaxes(new_rope, 0, 1), lengths))
    latent_out = jnp.swapaxes(latent_out, 0, 1)
    value_heads = value_weight.reshape(KVR, H, DV)
    attended = jnp.einsum("sbhk,khv->sbhv", latent_out.astype(jnp.float32), value_heads.astype(jnp.float32))
    return attended.astype(jnp.bfloat16).reshape(STEPS, BATCH, H * DV)
```

```python
import functools
import math

import jax
import jax.numpy as jnp
from jax import lax
from jax.experimental import pallas as pl
from jax.experimental.pallas import tpu as pltpu
from jax.sharding import PartitionSpec as P

QR = 1536
KVR = 512
DN = 128
DR = 64
DV = 128
CACHE = 2048
STEPS = 4
GROUPS = 32
HEADS = 4
RINGX = 4
DP = 8
KEYS = CACHE + 128
WIDE = KVR + 128
ROWS = GROUPS * HEADS * STEPS
BLOCK = 8
NB = GROUPS // BLOCK
BF = jnp.bfloat16
F32 = jnp.float32
MESH = pl.DeviceIdType.MESH


def iota(shape, dim):
    return lax.broadcasted_iota(jnp.int32, shape, dim)


def one_hot(source, columns):
    rows = source.shape[0]
    return jnp.where(iota((rows, columns), 1) == source, 1.0, 0.0).astype(BF)


def mm(a, b):
    return jnp.dot(a, b, preferred_element_type=F32)


def mm_t(a, b):
    return lax.dot_general(a, b, (((1,), (1,)), ((), ())), preferred_element_type=F32)


def kernel(
    q_ref, wq_ref, kw_ref, vw_ref, lat_hbm, rope_hbm, nl_ref, nr_ref, len_ref, out_ref,
    w32, k32, v32, small, pack, packv, qsend, rw, rv, rq, qnat, wqf, kvf, xs, send, recv, latx, kt,
    outs, back, lt, att,
    load_sem, snd, q_sem, w_sem, v_sem, a_sem, o_sem, xsnd, xrcv, vsnd, vrcv,
):
    dp = lax.axis_index("dp")
    me = lax.axis_index("head")
    xpos = dp // 2
    core = dp % 2
    right = ((xpos + 1) % RINGX) * 2 + core
    left = ((xpos + RINGX - 1) % RINGX) * 2 + core
    across = ((xpos + 2) % RINGX) * 2 + core
    other = xpos * 2 + (1 - core)

    def here(t):
        return {"dp": dp, "head": t}

    def peer(i):
        return lax.rem(me + i, GROUPS)

    barrier = pltpu.get_barrier_semaphore()

    def greet(i, carry):
        pl.semaphore_signal(barrier, inc=1, device_id=here(peer(i)), device_id_type=MESH)
        return carry

    lax.fori_loop(1, GROUPS, greet, 0)
    for d in (left, right, other):
        pl.semaphore_signal(barrier, inc=1, device_id={"dp": d, "head": me}, device_id_type=MESH)

    load_lat = pltpu.make_async_copy(lat_hbm.at[0], latx.at[pl.ds(0, CACHE)], load_sem.at[0])
    load_rope = pltpu.make_async_copy(rope_hbm.at[0], kt.at[pl.ds(KVR, DR), pl.ds(0, CACHE)], load_sem.at[1])
    load_lat.start()
    load_rope.start()

    for j in range(QR // 128):
        small[4 * j : 4 * j + 4, :] = q_ref[:, 128 * j : 128 * j + 128].astype(F32)
    qsend[...] = small[...].astype(BF)
    w32[6:8, :] = jnp.zeros((2, w32.shape[1]), F32)
    w32[0:6, :] = wq_ref[...].astype(F32)
    k32[0:6, :] = jnp.zeros((6, k32.shape[1]), F32)
    k32[6:8, :] = kw_ref[...].astype(F32)
    for b in range(HEADS):
        v32[2 * b : 2 * b + 2, :] = vw_ref[...].astype(F32)

    def pack_weights(t, carry):
        wide = pl.multiple_of(t * 768, 128)
        narrow = pl.multiple_of(t * 512, 128)
        parts = []
        for b in range(6):
            part = w32[:, pl.ds(wide + b * 128, 128)]
            if b < 4:
                part = part + k32[:, pl.ds(narrow + b * 128, 128)]
            parts.append(part)
        pack[t] = jnp.concatenate(parts, axis=0).astype(BF)
        return carry

    lax.fori_loop(0, GROUPS, pack_weights, 0)

    def pack_values(t, carry):
        narrow = pl.multiple_of(t * 512, 128)
        row = iota((8, 128), 0) // 2
        value = jnp.zeros((8, 128), F32)
        for b in range(HEADS):
            value = jnp.where(row == b, v32[:, pl.ds(narrow + b * 128, 128)], value)
        packv[t] = jnp.concatenate([value, jnp.zeros((8, 128), F32)], axis=0).astype(BF)
        return carry

    lax.fori_loop(0, GROUPS, pack_values, 0)

    pl.semaphore_wait(barrier, GROUPS - 1 + 3)

    mine = me // BLOCK

    def q_copy(i):
        return pltpu.make_async_remote_copy(qsend, rq.at[me], snd.at[0], q_sem.at[mine], here(peer(i)), MESH)

    def w_copy(i):
        t = peer(i)
        return pltpu.make_async_remote_copy(pack.at[t], rw.at[me], snd.at[1], w_sem.at[mine], here(t), MESH)

    def v_copy(i):
        t = peer(i)
        return pltpu.make_async_remote_copy(packv.at[t], rv.at[me], snd.at[2], v_sem.at[mine], here(t), MESH)

    def start_qw(i, carry):
        q_copy(i).start()
        w_copy(i).start()
        return carry

    def start_v(i, carry):
        v_copy(i).start()
        return carry

    own_q = pltpu.make_async_copy(qsend, rq.at[me], q_sem.at[mine])
    own_w = pltpu.make_async_copy(pack.at[me], rw.at[me], w_sem.at[mine])
    own_v = pltpu.make_async_copy(packv.at[me], rv.at[me], v_sem.at[mine])
    own_q.start()
    own_w.start()
    own_v.start()
    lax.fori_loop(1, GROUPS, start_qw, 0)
    lax.fori_loop(1, GROUPS, start_v, 0)

    def await_block(ref, sem, g):
        block = ref.at[pl.ds(g * BLOCK, BLOCK)]
        pltpu.make_async_copy(block, block, sem.at[g]).wait()

    small[0:8, :] = jnp.zeros((8, 128), F32)
    small[0:4, 0:DR] = nr_ref[...].astype(F32)
    fresh_rope = jnp.concatenate([small[0:8, :], jnp.zeros((120, 128), F32)], axis=0)
    kt[KVR:, CACHE:] = fresh_rope.T.astype(BF)
    kt[KVR + DR :, :CACHE] = jnp.zeros((128 - DR, CACHE), BF)
    for b in range(KVR // 128):
        small[0:8, :] = jnp.zeros((8, 128), F32)
        small[0:4, :] = nl_ref[:, b * 128 : b * 128 + 128].astype(F32)
        fresh = jnp.concatenate([small[0:8, :], jnp.zeros((120, 128), F32)], axis=0)
        latx[CACHE:, b * 128 : b * 128 + 128] = fresh.astype(BF)
    load_lat.wait()
    load_rope.wait()

    def turn(i, carry):
        at = pl.multiple_of(i * 128, 128)
        kt[0:KVR, pl.ds(at, 128)] = latx[pl.ds(at, 128), :].T
        return carry

    lax.fori_loop(0, KEYS // 128, turn, 0)

    o = iota((384, 1), 0)
    inside = o % 32
    q_order = one_hot((inside // 4) * 48 + (o // 32) * 4 + inside % 4, 384)
    for g in range(NB):
        await_block(rq, q_sem, g)
    arrived = jnp.concatenate([rq[g * BLOCK : (g + 1) * BLOCK].reshape(384, 128) for g in range(NB)], axis=1)
    ordered = mm(q_order, arrived).astype(BF)
    for j in range(QR // 128):
        for g in range(NB):
            qnat[g * 32 : g * 32 + 32, j * 128 : j * 128 + 128] = ordered[j * 32 : j * 32 + 32, g * 128 : g * 128 + 128]

    u = o % 64
    sixth = (u * 43) >> 8
    from_query = sixth * 48 + (o // 64) * 8 + (u - sixth * 6)
    from_key = ((u - 48) // 2) * 48 + (o // 64) * 8 + 6 + (u % 2)
    w_order = one_hot(jnp.where(u < 48, from_query, from_key), 384)
    for g in range(NB):
        await_block(rw, w_sem, g)
    arrived = jnp.concatenate([rw[g * BLOCK : (g + 1) * BLOCK].reshape(384, 128) for g in range(NB)], axis=1)
    ordered = mm(w_order, arrived).astype(BF)
    for b in range(6):
        for g in range(NB):
            lanes = slice(g * 128, g * 128 + 128)
            wqf[dp, g * 48 : g * 48 + 48, b * 128 : b * 128 + 128] = ordered[b * 64 : b * 64 + 48, lanes]
            if b < 4:
                kvf[dp, g * 16 : g * 16 + 16, b * 128 : b * 128 + 128] = ordered[b * 64 + 48 : b * 64 + 64, lanes]

    def ring(pieces, ssem, rsem):
        count = len(pieces)

        def copy(k, p, owner, to, part=None):
            ref, first, rows = pieces[p]
            if part is not None:
                rows = rows // 2
                first = first + part * rows
            view = ref.at[owner, pl.ds(first, rows)]
            slot = k * count + p
            return pltpu.make_async_remote_copy(
                view, view, ssem.at[slot], rsem.at[slot], {"dp": to, "head": me}, MESH
            )

        every = range(count)

        def begin():
            for p in every:
                copy(0, p, dp, right, 0).start()
                copy(1, p, dp, left, 1).start()
            for p in every:
                copy(2, p, dp, right, 1).start()
                copy(3, p, dp, left, 0).start()
            for p in every:
                copy(4, p, dp, other).start()

        def forward():
            for p in every:
                copy(0, p, left, right, 0).wait_recv()
                copy(5, p, left, right, 0).start()
                copy(1, p, right, left, 1).wait_recv()
                copy(6, p, right, left, 1).start()

        def neighbours():
            for p in every:
                copy(2, p, left, right, 1).wait_recv()
                copy(7, p, left, other).start()
                copy(3, p, right, left, 0).wait_recv()
                copy(8, p, right, other).start()

        def far():
            for p in every:
                copy(5, p, across, right, 0).wait_recv()
                copy(6, p, across, left, 1).wait_recv()
                copy(9, p, across, other).start()

        def finish():
            sib = 1 - 2 * core
            for p in every:
                copy(4, p, dp + sib, other).wait_recv()
                copy(7, p, left + sib, other).wait_recv()
                copy(8, p, right + sib, other).wait_recv()
                copy(9, p, across + sib, other).wait_recv()
            for p in every:
                for k, part in ((0, 0), (1, 1), (2, 1), (3, 0), (4, None), (5, 0), (6, 1), (7, None), (8, None), (9, None)):
                    copy(k, p, dp, right, part).wait_send()

        return begin, forward, neighbours, far, finish

    for step in ring([(wqf, 0, 192), (kvf, 0, 64)], xsnd, xrcv):
        step()

    projected = mm(qnat[...], wqf[...].reshape(QR, 768))
    xs[:, KVR:] = jnp.zeros((ROWS, WIDE - KVR), BF)
    for h in range(HEADS):
        at = h * (DN + DR)
        plain = projected[:, at : at + DN].astype(BF)
        keys = kvf[:, 0:64, h * DN : (h + 1) * DN].reshape(KVR, DN)
        xs[h * 128 : h * 128 + 128, 0:KVR] = mm_t(plain, keys).astype(BF)
        xs[h * 128 : h * 128 + 128, KVR : KVR + DR] = projected[:, at + DN : at + DN + DR].astype(BF)

    o = iota((128, 1), 0)
    by_seq = one_hot(((o // 4) % 4) * 32 + (o // 16) * 4 + o % 4, 128)
    by_head = one_hot(((o // 4) % 8) * 16 + (o // 32) * 4 + o % 4, 128)
    by_step = one_hot((o % 32) * 4 + o // 32, 128)

    def send_queries(k, carry):
        g = lax.rem(mine + k, NB)
        stacked = jnp.concatenate(
            [xs[pl.ds(pl.multiple_of(h * 128 + g * 32, 32), 32), :] for h in range(HEADS)], axis=0
        )
        send[pl.ds(g * BLOCK, BLOCK)] = mm(by_seq, stacked).astype(BF).reshape(BLOCK, 16, WIDE)

        def one(j, c):
            t = g * BLOCK + j

            @pl.when(t != me)
            def _():
                pltpu.make_async_remote_copy(
                    send.at[t], recv.at[me], snd.at[3], a_sem.at[mine], here(t), MESH
                ).start()

            return c

        lax.fori_loop(0, BLOCK, one, 0)
        return carry

    lax.fori_loop(0, NB, send_queries, 0)
    own_a = pltpu.make_async_copy(send.at[me], recv.at[me], a_sem.at[mine])
    own_a.start()

    o = iota((64, 1), 0)
    v_order = one_hot(((o % 16) // 2) * 16 + (o // 16) * 2 + o % 2, 128)
    for g in range(NB):
        await_block(rv, v_sem, g)
    arrived = jnp.concatenate([rv[g * BLOCK : (g + 1) * BLOCK].reshape(128, 128) for g in range(NB)], axis=1)
    ordered = mm(v_order, arrived).astype(BF)
    for b in range(4):
        for g in range(NB):
            kvf[dp, 64 + g * 16 : 64 + g * 16 + 16, b * 128 : b * 128 + 128] = ordered[
                b * 16 : b * 16 + 16, g * 128 : g * 128 + 128
            ]
    v_steps = ring([(kvf, 64, 64)], vsnd, vrcv)
    v_steps[0]()
    v_steps[1]()
    v_steps[2]()

    length = len_ref[0]
    factor = (DN + DR) ** -0.5 * math.log2(math.e)
    half = NB // 2
    chunk = ROWS // half

    def attend(r):
        for e in range(half):
            await_block(recv, a_sem, r * half + e)
        rows = recv[pl.ds(r * 16, 16)].reshape(chunk, WIDE)
        scores = mm(rows, kt[...]) * factor
        slot = iota((chunk, KEYS), 1)
        step = iota((chunk, 1), 0) % STEPS
        last = jnp.maximum(length - 1, 0)
        keep = (slot <= last) | ((slot >= CACHE) & (slot <= CACHE + step))
        scores = jnp.where(keep, scores, -1e30)
        top = jnp.max(scores, axis=1, keepdims=True)
        raised = jnp.exp2(scores - top)
        total = jnp.sum(raised, axis=1, keepdims=True)
        mixed = mm(raised.astype(BF), latx[...]) / total
        outs[pl.ds(r * 16, 16)] = mixed.astype(BF).reshape(16, 16, KVR)

        def one(j, c):
            t = r * 16 + j

            @pl.when(t != me)
            def _():
                pltpu.make_async_remote_copy(
                    outs.at[t], back.at[me], snd.at[4], o_sem.at[mine], here(t), MESH
                ).start()

            return c

        lax.fori_loop(0, 16, one, 0)

    first = me // 16

    def attend_one(k, carry):
        attend(lax.rem(first + k, half))
        return carry

    lax.fori_loop(0, half, attend_one, 0)
    own_o = pltpu.make_async_copy(outs.at[me], back.at[me], o_sem.at[mine])
    own_o.start()
    v_steps[3]()
    v_steps[4]()

    def collect(g, carry):
        await_block(back, o_sem, g)
        block = mm(by_head, back[pl.ds(g * BLOCK, BLOCK)].reshape(128, KVR)).astype(BF)
        for h in range(HEADS):
            lt[h, pl.ds(pl.multiple_of(g * 32, 32), 32), :] = block[h * 32 : h * 32 + 32]
        return carry

    lax.fori_loop(0, NB, collect, 0)
    for h in range(HEADS):
        values = kvf[:, 64:128, h * DV : (h + 1) * DV].reshape(KVR, DV)
        att[:, h * DV : (h + 1) * DV] = mm(lt[h], values).astype(BF)
    out_ref[...] = mm(by_step, att[...]).astype(BF).reshape(STEPS, GROUPS, HEADS * DV)

    def await_sent(ref, k):
        block = ref.at[pl.ds(0, GROUPS - 1)]
        pltpu.make_async_copy(block, block, snd.at[k]).wait()

    await_sent(rq, 0)
    await_sent(pack, 1)
    await_sent(packv, 2)
    await_sent(send, 3)
    await_sent(outs, 4)


def body(
    query_latent,
    query_weight,
    key_weight,
    value_weight,
    cache_latent,
    cache_rope,
    new_latent,
    new_rope,
    lengths,
):
    vmem = pl.BlockSpec(memory_space=pltpu.VMEM)
    anywhere = pl.BlockSpec(memory_space=pl.ANY)
    smem = pl.BlockSpec(memory_space=pltpu.SMEM)
    dma = pltpu.SemaphoreType.DMA
    return pl.pallas_call(
        kernel,
        out_shape=jax.ShapeDtypeStruct((STEPS, GROUPS, HEADS * DV), BF),
        in_specs=[vmem, vmem, vmem, vmem, anywhere, anywhere, vmem, vmem, smem],
        out_specs=vmem,
        scratch_shapes=[
            pltpu.VMEM((8, GROUPS * 768), F32),
            pltpu.VMEM((8, GROUPS * 512), F32),
            pltpu.VMEM((8, GROUPS * 512), F32),
            pltpu.VMEM((48, 128), F32),
            pltpu.VMEM((GROUPS, 48, 128), BF),
            pltpu.VMEM((GROUPS, 16, 128), BF),
            pltpu.VMEM((48, 128), BF),
            pltpu.VMEM((GROUPS, 48, 128), BF),
            pltpu.VMEM((GROUPS, 16, 128), BF),
            pltpu.VMEM((GROUPS, 48, 128), BF),
            pltpu.VMEM((128, QR), BF),
            pltpu.VMEM((DP, 192, 768), BF),
            pltpu.VMEM((DP, 128, 512), BF),
            pltpu.VMEM((ROWS, WIDE), BF),
            pltpu.VMEM((GROUPS, 16, WIDE), BF),
            pltpu.VMEM((GROUPS, 16, WIDE), BF),
            pltpu.VMEM((KEYS, KVR), BF),
            pltpu.VMEM((WIDE, KEYS), BF),
            pltpu.VMEM((GROUPS, 16, KVR), BF),
            pltpu.VMEM((GROUPS, 16, KVR), BF),
            pltpu.VMEM((HEADS, 128, KVR), BF),
            pltpu.VMEM((128, HEADS * DV), BF),
            dma((2,)),
            dma((5,)),
            dma((NB,)),
            dma((NB,)),
            dma((NB,)),
            dma((NB,)),
            dma((NB,)),
            dma((20,)),
            dma((20,)),
            dma((10,)),
            dma((10,)),
        ],
        compiler_params=pltpu.CompilerParams(
            collective_id=0, has_side_effects=True, vmem_limit_bytes=56 * 1024 * 1024
        ),
    )(
        query_latent.reshape(STEPS, QR),
        query_weight,
        key_weight,
        value_weight,
        cache_latent,
        cache_rope,
        new_latent.reshape(STEPS, KVR),
        new_rope.reshape(STEPS, DR),
        lengths,
    )


def solution(mesh):
    placed = (
        P(None, ("dp", "head"), None),
        P(("dp", "head"), None),
        P(("dp", "head"), None),
        P(("dp", "head"), None),
        P(("dp", "head"), None, None),
        P(("dp", "head"), None, None),
        P(None, ("dp", "head"), None),
        P(None, ("dp", "head"), None),
        P(("dp", "head")),
    )
    return jax.shard_map(
        body, mesh=mesh, in_specs=placed, out_specs=P(None, "dp", "head"), check_vma=False
    )
```

```python
import functools
import math

import jax
import jax.numpy as jnp
from jax import lax
from jax.experimental import pallas as pl
from jax.experimental.pallas import tpu as pltpu
from jax.sharding import PartitionSpec as P

QR = 1536
KVR = 512
DN = 128
DR = 64
DV = 128
CACHE = 2048
STEPS = 4
GROUPS = 32
HEADS = 4
RINGX = 4
RINGY = 4
RINGZ = 8
DP = 8
KEYS = CACHE + 128
WIDE = KVR + 128
ROWS = GROUPS * HEADS * STEPS
BLOCK = 8
NB = GROUPS // BLOCK
BF = jnp.bfloat16
F32 = jnp.float32
MESH = pl.DeviceIdType.MESH


def iota(shape, dim):
    return lax.broadcasted_iota(jnp.int32, shape, dim)


def one_hot(source, columns):
    rows = source.shape[0]
    return jnp.where(iota((rows, columns), 1) == source, 1.0, 0.0).astype(BF)


def mm(a, b):
    return jnp.dot(a, b, preferred_element_type=F32)


def mm_t(a, b):
    return lax.dot_general(a, b, (((1,), (1,)), ((), ())), preferred_element_type=F32)


def kernel(
    q_ref, wq_ref, kw_ref, vw_ref, lat_hbm, rope_hbm, nl_ref, nr_ref, len_ref, out_ref,
    w32, k32, v32, small, packa, packb, packv, qsend, rwa, rwb, rv, rq, qnat, wa, wb, ka, kb, vf,
    absq, posq, senda, sendb, recva, recvb, lhs, latx, kt, outs, back, lt, att,
    load_sem, snd, rcv, xsnd, xrcv, ysnd, yrcv, vsnd, vrcv,
):
    dp = lax.axis_index("dp")
    me = lax.axis_index("head")
    xpos = dp // 2
    core = dp % 2
    right = ((xpos + 1) % RINGX) * 2 + core
    left = ((xpos + RINGX - 1) % RINGX) * 2 + core
    across = ((xpos + 2) % RINGX) * 2 + core
    other = xpos * 2 + (1 - core)
    zpos = me // RINGY
    ypos = me % RINGY
    diagonal = (ypos + 2 * RINGY - zpos) % RINGY
    slot = diagonal * RINGZ + zpos

    def here(t):
        return {"dp": dp, "head": t}

    def peer(i):
        d = (diagonal + i // RINGZ) % RINGY
        z = (zpos + i) % RINGZ
        return d * RINGZ + z, z * RINGY + (d + z) % RINGY

    barrier = pltpu.get_barrier_semaphore()

    def greet(i, carry):
        pl.semaphore_signal(barrier, inc=1, device_id=here(peer(i)[1]), device_id_type=MESH)
        return carry

    lax.fori_loop(1, GROUPS, greet, 0)
    for d in (left, right, other):
        pl.semaphore_signal(barrier, inc=1, device_id={"dp": d, "head": me}, device_id_type=MESH)

    load_lat = pltpu.make_async_copy(lat_hbm.at[0], latx.at[pl.ds(0, CACHE)], load_sem.at[0])
    load_rope = pltpu.make_async_copy(rope_hbm.at[0], kt.at[pl.ds(KVR, DR), pl.ds(0, CACHE)], load_sem.at[1])
    load_lat.start()
    load_rope.start()

    w32[6:8, :] = jnp.zeros((2, w32.shape[1]), F32)
    w32[0:6, :] = wq_ref[...].astype(F32)
    k32[0:6, :] = jnp.zeros((6, k32.shape[1]), F32)
    k32[6:8, :] = kw_ref[...].astype(F32)

    def pack_weights(t, carry):
        wide = pl.multiple_of(t * 768, 128)
        narrow = pl.multiple_of(t * 512, 128)
        p = [w32[:, pl.ds(wide + b * 128, 128)] for b in range(6)]
        k = [k32[:, pl.ds(narrow + b * 128, 128)] for b in range(4)]
        low = iota((8, 128), 1) < DR
        positions = jnp.where(low, p[4], p[5])
        swapped = jnp.where(low, p[5], p[4])
        packa[t] = jnp.concatenate([p[0] + k[0], p[1] + k[1], p[2], positions], axis=0).astype(BF)
        packb[t] = jnp.concatenate([p[3] + k[2], swapped + k[3]], axis=0).astype(BF)
        return carry

    lax.fori_loop(0, GROUPS, pack_weights, 0)
    for j in range(QR // 128):
        small[4 * j : 4 * j + 4, :] = q_ref[:, 128 * j : 128 * j + 128].astype(F32)
    qsend[...] = small[...].astype(BF)
    for b in range(HEADS):
        v32[2 * b : 2 * b + 2, :] = vw_ref[...].astype(F32)

    def pack_values(t, carry):
        narrow = pl.multiple_of(t * 512, 128)
        row = iota((8, 128), 0) // 2
        value = jnp.zeros((8, 128), F32)
        for b in range(HEADS):
            value = jnp.where(row == b, v32[:, pl.ds(narrow + b * 128, 128)], value)
        packv[t] = jnp.concatenate([value, jnp.zeros((8, 128), F32)], axis=0).astype(BF)
        return carry

    lax.fori_loop(0, GROUPS, pack_values, 0)

    pl.semaphore_wait(barrier, GROUPS - 1 + 3)

    def scatter(source, target, k, place):
        def one(i, carry):
            s, t = peer(i)
            pltpu.make_async_remote_copy(
                source(s, t), target.at[place], snd.at[k], rcv.at[k], here(t), MESH
            ).start()
            return carry

        pltpu.make_async_copy(source(slot, me), target.at[place], rcv.at[k]).start()
        lax.fori_loop(1, GROUPS, one, 0)

    def arrive(target, k):
        pltpu.make_async_copy(target, target, rcv.at[k]).wait()

    scatter(lambda s, t: packa.at[t], rwa, 0, me)
    scatter(lambda s, t: packb.at[t], rwb, 1, me)
    scatter(lambda s, t: qsend, rq, 2, slot)
    scatter(lambda s, t: packv.at[t], rv, 3, me)

    small[0:8, :] = jnp.zeros((8, 128), F32)
    small[0:4, 0:DR] = nr_ref[...].astype(F32)
    fresh_rope = jnp.concatenate([small[0:8, :], jnp.zeros((120, 128), F32)], axis=0)
    kt[KVR:, CACHE:] = fresh_rope.T.astype(BF)
    kt[KVR + DR :, :CACHE] = jnp.zeros((128 - DR, CACHE), BF)
    for b in range(KVR // 128):
        small[0:8, :] = jnp.zeros((8, 128), F32)
        small[0:4, :] = nl_ref[:, b * 128 : b * 128 + 128].astype(F32)
        fresh = jnp.concatenate([small[0:8, :], jnp.zeros((120, 128), F32)], axis=0)
        latx[CACHE:, b * 128 : b * 128 + 128] = fresh.astype(BF)
    load_lat.wait()
    load_rope.wait()

    def turn(i, carry):
        at = pl.multiple_of(i * 128, 128)
        kt[0:KVR, pl.ds(at, 128)] = latx[pl.ds(at, 128), :].T
        return carry

    lax.fori_loop(0, KEYS // 128, turn, 0)

    def weight_order(blocks):
        o = iota((blocks * 64, 1), 0)
        u = o % 64
        sixth = (u * 43) >> 8
        from_query = sixth * (blocks * 8) + (o // 64) * 8 + (u - sixth * 6)
        from_key = ((u - 48) // 2) * (blocks * 8) + (o // 64) * 8 + 6 + (u % 2)
        return one_hot(jnp.where(u < 48, from_query, from_key), blocks * 64)

    order_a = weight_order(4)
    order_b = weight_order(2)
    o = iota((384, 1), 0)
    inside = o % 32
    q_order = one_hot((inside // 4) * 48 + (o // 32) * 4 + inside % 4, 384)
    o = iota((128, 1), 0)
    by_slot = one_hot(((o // 4) % 4) * 32 + (o // 16) * 4 + o % 4, 128)
    by_part = one_hot(((o // 4) % 8) * 16 + (o // 32) * 4 + o % 4, 128)
    halves = one_hot(((o // 8) % 8) * 16 + (o // 64) * 8 + o % 8, 128)
    unhalve = one_hot(((o // 8) % 2) * 64 + (o // 16) * 8 + o % 8, 128)
    sequence = o % 32
    home = ((sequence % 4 + 8 - sequence // 4) % 4) * 8 + sequence // 4
    by_step = one_hot(home * 4 + o // 32, 128)

    def rearranged(order, ref, rows):
        blocks = [ref[g * BLOCK : (g + 1) * BLOCK].reshape(BLOCK * rows, 128) for g in range(NB)]
        return mm(order, jnp.concatenate(blocks, axis=1)).astype(BF)

    def compact(order, ref, blocks, weights, keys):
        ordered = rearranged(order, ref, blocks * 8)
        for b in range(blocks):
            for g in range(NB):
                lanes = slice(g * 128, g * 128 + 128)
                weights[dp, g * 48 : g * 48 + 48, b * 128 : b * 128 + 128] = ordered[b * 64 : b * 64 + 48, lanes]
                if b < 2:
                    keys[dp, g * 16 : g * 16 + 16, b * 128 : b * 128 + 128] = ordered[b * 64 + 48 : b * 64 + 64, lanes]

    def ring(pieces, ssem, rsem):
        count = len(pieces)

        def copy(k, p, owner, to, part=None):
            ref = pieces[p]
            rows = ref.shape[1]
            first = 0
            if part is not None:
                rows = rows // 2
                first = part * rows
            view = ref.at[owner, pl.ds(first, rows)]
            at = k * count + p
            return pltpu.make_async_remote_copy(view, view, ssem.at[at], rsem.at[at], {"dp": to, "head": me}, MESH)

        every = range(count)

        def begin():
            for p in every:
                copy(0, p, dp, right, 0).start()
                copy(1, p, dp, left, 1).start()
            for p in every:
                copy(2, p, dp, right, 1).start()
                copy(3, p, dp, left, 0).start()
            for p in every:
                copy(4, p, dp, other).start()

        def forward():
            for p in every:
                copy(0, p, left, right, 0).wait_recv()
                copy(5, p, left, right, 0).start()
                copy(1, p, right, left, 1).wait_recv()
                copy(6, p, right, left, 1).start()

        def neighbours():
            for p in every:
                copy(2, p, left, right, 1).wait_recv()
                copy(7, p, left, other).start()
                copy(3, p, right, left, 0).wait_recv()
                copy(8, p, right, other).start()

        def far():
            for p in every:
                copy(5, p, across, right, 0).wait_recv()
                copy(6, p, across, left, 1).wait_recv()
                copy(9, p, across, other).start()

        def finish():
            sib = 1 - 2 * core
            for p in every:
                copy(4, p, dp + sib, other).wait_recv()
                copy(7, p, left + sib, other).wait_recv()
                copy(8, p, right + sib, other).wait_recv()
                copy(9, p, across + sib, other).wait_recv()

        def close():
            for p in every:
                for k, part in ((0, 0), (1, 1), (2, 1), (3, 0), (4, None), (5, 0), (6, 1), (7, None), (8, None), (9, None)):
                    copy(k, p, dp, right, part).wait_send()

        return begin, forward, neighbours, far, finish, close

    ring_a = ring([wa, ka], xsnd, xrcv)
    ring_b = ring([wb, kb], ysnd, yrcv)
    ring_v = ring([vf], vsnd, vrcv)

    arrive(rwa, 0)
    compact(order_a, rwa, 4, wa, ka)
    ring_a[0]()
    arrive(rwb, 1)
    compact(order_b, rwb, 2, wb, kb)
    ring_a[1]()
    ring_b[0]()
    ring_a[2]()

    arrive(rq, 2)
    ordered = rearranged(q_order, rq, 48)
    for j in range(QR // 128):
        for g in range(NB):
            qnat[g * 32 : g * 32 + 32, j * 128 : j * 128 + 128] = ordered[j * 32 : j * 32 + 32, g * 128 : g * 128 + 128]
    ring_a[3]()
    ring_a[4]()

    def absorb(h, plain, keys):
        lanes = slice((h % 2) * DN, (h % 2) * DN + DN)
        absq[h * 128 : h * 128 + 128, :] = mm_t(plain.astype(BF), keys[:, :, lanes].reshape(KVR, DN)).astype(BF)

    def spread(pair, with_position, send, recv, k):
        for d in range(NB):
            stacked = [
                absq[h * 128 + d * 32 : h * 128 + d * 32 + 32, e * 256 : e * 256 + 256]
                for e in range(2)
                for h in (2 * pair, 2 * pair + 1)
            ]
            stacked = jnp.concatenate(stacked, axis=0)
            if with_position:
                position = [posq[h * 128 + d * 32 : h * 128 + d * 32 + 32, :] for h in range(HEADS)]
                stacked = jnp.concatenate([stacked, jnp.concatenate(position, axis=0)], axis=1)
            send[d * BLOCK : (d + 1) * BLOCK] = mm(by_slot, stacked).astype(BF).reshape(BLOCK, 16, stacked.shape[1])
        scatter(lambda s, t: send.at[s], recv, k, slot)

    projected = mm(qnat[...], wa[...].reshape(QR, 512))
    absorb(0, projected[:, 0:128], ka)
    absorb(1, projected[:, 192:320], ka)
    posq[:, DR:] = jnp.zeros((ROWS, 128 - DR), BF)
    for h, at in enumerate((128, 320, 384, 448)):
        posq[h * 128 : h * 128 + 128, 0:DR] = projected[:, at : at + DR].astype(BF)
    spread(0, True, senda, recva, 4)

    for step in ring_b[1:5]:
        step()
    projected = mm(qnat[...], wb[...].reshape(QR, 256))
    absorb(2, projected[:, 0:128], kb)
    absorb(3, pltpu.roll(projected[:, 128:256], DR, 1), kb)
    spread(1, False, sendb, recvb, 5)

    o = iota((64, 1), 0)
    v_order = one_hot(((o % 16) // 2) * 16 + (o // 16) * 2 + o % 2, 128)
    arrive(rv, 3)
    ordered = rearranged(v_order, rv, 16)
    for b in range(4):
        for g in range(NB):
            vf[dp, g * 16 : g * 16 + 16, b * 128 : b * 128 + 128] = ordered[b * 16 : b * 16 + 16, g * 128 : g * 128 + 128]
    ring_v[0]()
    ring_v[1]()

    length = len_ref[0]
    factor = (DN + DR) ** -0.5 * math.log2(math.e)
    chunk = ROWS // 2

    def attend(pair):
        scores = mm(lhs[pair], kt[...]) * factor
        key = iota((chunk, KEYS), 1)
        step = iota((chunk, 1), 0) % STEPS
        last = jnp.maximum(length - 1, 0)
        keep = (key <= last) | ((key >= CACHE) & (key <= CACHE + step))
        scores = jnp.where(keep, scores, -1e30)
        top = jnp.max(scores, axis=1, keepdims=True)
        raised = jnp.exp2(scores - top)
        total = jnp.sum(raised, axis=1, keepdims=True)
        mixed = (mm(raised.astype(BF), latx[...]) / total).astype(BF)
        for d in range(NB):
            stacked = jnp.concatenate(
                [mixed[d * 64 : d * 64 + 64, 0:256], mixed[d * 64 : d * 64 + 64, 256:512]], axis=0
            )
            outs[pair, d * BLOCK : (d + 1) * BLOCK] = mm(unhalve, stacked).astype(BF).reshape(BLOCK, 16, 256)
        scatter(lambda s, t: outs.at[pair, s], back.at[pair], 6 + pair, slot)

    arrive(recva, 4)
    for d in range(NB):
        block = mm(halves, recva[d * BLOCK : (d + 1) * BLOCK].reshape(128, 384)).astype(BF)
        rows = slice(d * 64, d * 64 + 64)
        lhs[0, rows, 0:256] = block[0:64, 0:256]
        lhs[0, rows, 256:512] = block[64:128, 0:256]
        lhs[0, rows, 512:640] = block[0:64, 256:384]
        lhs[1, rows, 512:640] = block[64:128, 256:384]
    attend(0)
    ring_v[2]()
    ring_v[3]()
    arrive(recvb, 5)
    for d in range(NB):
        block = mm(halves, recvb[d * BLOCK : (d + 1) * BLOCK].reshape(128, 256)).astype(BF)
        rows = slice(d * 64, d * 64 + 64)
        lhs[1, rows, 0:256] = block[0:64]
        lhs[1, rows, 256:512] = block[64:128]
    attend(1)
    ring_v[4]()

    for pair in range(2):
        arrive(back.at[pair], 6 + pair)
        for d in range(NB):
            block = mm(by_part, back[pair, d * BLOCK : (d + 1) * BLOCK].reshape(128, 256)).astype(BF)
            for e in range(2):
                for h in range(2):
                    at = (e * 2 + h) * 32
                    lt[h, d * 32 : d * 32 + 32, e * 256 : e * 256 + 256] = block[at : at + 32]
        for h in range(2):
            lanes = slice((2 * pair + h) * DV, (2 * pair + h + 1) * DV)
            att[:, lanes] = mm(lt[h], vf[:, :, lanes].reshape(KVR, DV)).astype(BF)
    out_ref[...] = mm(by_step, att[...]).astype(BF).reshape(STEPS, GROUPS, HEADS * DV)

    for k, ref in enumerate((packa, packb, rq, packv, senda, sendb, outs.at[0], outs.at[1])):
        block = ref.at[pl.ds(0, GROUPS - 1)]
        pltpu.make_async_copy(block, block, snd.at[k]).wait()
    for steps in (ring_a, ring_b, ring_v):
        steps[5]()


def body(
    query_latent,
    query_weight,
    key_weight,
    value_weight,
    cache_latent,
    cache_rope,
    new_latent,
    new_rope,
    lengths,
):
    vmem = pl.BlockSpec(memory_space=pltpu.VMEM)
    anywhere = pl.BlockSpec(memory_space=pl.ANY)
    smem = pl.BlockSpec(memory_space=pltpu.SMEM)
    dma = pltpu.SemaphoreType.DMA
    return pl.pallas_call(
        kernel,
        out_shape=jax.ShapeDtypeStruct((STEPS, GROUPS, HEADS * DV), BF),
        in_specs=[vmem, vmem, vmem, vmem, anywhere, anywhere, vmem, vmem, smem],
        out_specs=vmem,
        scratch_shapes=[
            pltpu.VMEM((8, GROUPS * 768), F32),
            pltpu.VMEM((8, GROUPS * 512), F32),
            pltpu.VMEM((8, GROUPS * 512), F32),
            pltpu.VMEM((48, 128), F32),
            pltpu.VMEM((GROUPS, 32, 128), BF),
            pltpu.VMEM((GROUPS, 16, 128), BF),
            pltpu.VMEM((GROUPS, 16, 128), BF),
            pltpu.VMEM((48, 128), BF),
            pltpu.VMEM((GROUPS, 32, 128), BF),
            pltpu.VMEM((GROUPS, 16, 128), BF),
            pltpu.VMEM((GROUPS, 16, 128), BF),
            pltpu.VMEM((GROUPS, 48, 128), BF),
            pltpu.VMEM((128, QR), BF),
            pltpu.VMEM((DP, 192, 512), BF),
            pltpu.VMEM((DP, 192, 256), BF),
            pltpu.VMEM((DP, 64, 256), BF),
            pltpu.VMEM((DP, 64, 256), BF),
            pltpu.VMEM((DP, 64, 512), BF),
            pltpu.VMEM((ROWS, KVR), BF),
            pltpu.VMEM((ROWS, 128), BF),
            pltpu.VMEM((GROUPS, 16, 384), BF),
            pltpu.VMEM((GROUPS, 16, 256), BF),
            pltpu.VMEM((GROUPS, 16, 384), BF),
            pltpu.VMEM((GROUPS, 16, 256), BF),
            pltpu.VMEM((2, ROWS // 2, WIDE), BF),
            pltpu.VMEM((KEYS, KVR), BF),
            pltpu.VMEM((WIDE, KEYS), BF),
            pltpu.VMEM((2, GROUPS, 16, 256), BF),
            pltpu.VMEM((2, GROUPS, 16, 256), BF),
            pltpu.VMEM((2, 128, KVR), BF),
            pltpu.VMEM((128, HEADS * DV), BF),
            dma((2,)),
            dma((8,)),
            dma((8,)),
            dma((20,)),
            dma((20,)),
            dma((20,)),
            dma((20,)),
            dma((10,)),
            dma((10,)),
        ],
        compiler_params=pltpu.CompilerParams(
            collective_id=0, has_side_effects=True, vmem_limit_bytes=56 * 1024 * 1024
        ),
    )(
        query_latent.reshape(STEPS, QR),
        query_weight,
        key_weight,
        value_weight,
        cache_latent,
        cache_rope,
        new_latent.reshape(STEPS, KVR),
        new_rope.reshape(STEPS, DR),
        lengths,
    )


def solution(mesh):
    placed = (
        P(None, ("dp", "head"), None),
        P(("dp", "head"), None),
        P(("dp", "head"), None),
        P(("dp", "head"), None),
        P(("dp", "head"), None, None),
        P(("dp", "head"), None, None),
        P(None, ("dp", "head"), None),
        P(None, ("dp", "head"), None),
        P(("dp", "head")),
    )
    return jax.shard_map(
        body, mesh=mesh, in_specs=placed, out_specs=P(None, "dp", "head"), check_vma=False
    )
```

```python
import functools
import math

import jax
import jax.numpy as jnp
from jax import lax
from jax.experimental import pallas as pl
from jax.experimental.pallas import tpu as pltpu
from jax.sharding import PartitionSpec as P

QR = 1536
KVR = 512
DN = 128
DR = 64
DV = 128
CACHE = 2048
STEPS = 4
GROUPS = 32
HEADS = 4
RINGX = 4
RINGY = 4
RINGZ = 8
DP = 8
KEYS = CACHE + 128
WIDE = KVR + 128
ROWS = GROUPS * HEADS * STEPS
BLOCK = 8
NB = GROUPS // BLOCK
BF = jnp.bfloat16
F32 = jnp.float32
MESH = pl.DeviceIdType.MESH


def iota(shape, dim):
    return lax.broadcasted_iota(jnp.int32, shape, dim)


def one_hot(source, columns):
    rows = source.shape[0]
    return jnp.where(iota((rows, columns), 1) == source, 1.0, 0.0).astype(BF)


def mm(a, b):
    return jnp.dot(a, b, preferred_element_type=F32)


def mm_t(a, b):
    return lax.dot_general(a, b, (((1,), (1,)), ((), ())), preferred_element_type=F32)


def kernel(
    q_ref, wq_ref, kw_ref, vw_ref, lat_hbm, rope_hbm, nl_ref, nr_ref, len_ref, out_ref,
    w32, k32, v32, small, packr, packa, packb, packv, qsend, rwr, rwa, rwb, rv, rq, qnat, wr, wa, wb, ka, kb, vf,
    absq, posq, sendr, senda, sendb, recvr, recva, recvb, lhs, latx, kt, outs, back, lt, att,
    load_sem, snd, rcv, rrcvd, arcvd, brcvd, qsnd, qrcv, rsnd, rrcv, xsnd, xrcv, ysnd, yrcv, vsnd, vrcv,
):
    dp = lax.axis_index("dp")
    me = lax.axis_index("head")
    xpos = dp // 2
    core = dp % 2
    right = ((xpos + 1) % RINGX) * 2 + core
    left = ((xpos + RINGX - 1) % RINGX) * 2 + core
    across = ((xpos + 2) % RINGX) * 2 + core
    other = xpos * 2 + (1 - core)
    zpos = me // RINGY
    ypos = me % RINGY
    diagonal = (ypos + 2 * RINGY - zpos) % RINGY
    slot = diagonal * RINGZ + zpos

    def here(t):
        return {"dp": dp, "head": t}

    turns = [lax.rem(diagonal + k, RINGY) for k in range(RINGY)]
    planes = [lax.rem(zpos + i, RINGZ) for i in range(RINGZ)]
    partners = [(d * RINGZ + z, z * RINGY + lax.rem(d + z, RINGY)) for d in turns for z in planes]

    barrier = pltpu.get_barrier_semaphore()

    for _, t in partners[1:]:
        pl.semaphore_signal(barrier, inc=1, device_id=here(t), device_id_type=MESH)
    for d in (left, right, other):
        pl.semaphore_signal(barrier, inc=1, device_id={"dp": d, "head": me}, device_id_type=MESH)

    load_lat = pltpu.make_async_copy(lat_hbm.at[0], latx.at[pl.ds(0, CACHE)], load_sem.at[0])
    load_rope = pltpu.make_async_copy(rope_hbm.at[0], kt.at[pl.ds(KVR, DR), pl.ds(0, CACHE)], load_sem.at[1])
    load_lat.start()
    load_rope.start()

    w32[6:8, :] = jnp.zeros((2, w32.shape[1]), F32)
    w32[0:6, :] = wq_ref[...].astype(F32)
    k32[0:6, :] = jnp.zeros((6, k32.shape[1]), F32)
    k32[6:8, :] = kw_ref[...].astype(F32)

    def pack_weights(t, carry):
        wide = pl.multiple_of(t * 768, 128)
        narrow = pl.multiple_of(t * 512, 128)
        p = [w32[:, pl.ds(wide + b * 128, 128)] for b in range(6)]
        k = [k32[:, pl.ds(narrow + b * 128, 128)] for b in range(4)]
        low = iota((8, 128), 1) < DR
        positions = jnp.where(low, p[4], p[5])
        swapped = jnp.where(low, p[5], p[4])
        first = jnp.where(low, p[1], p[2])
        exchanged = jnp.where(low, p[2], p[1])
        packr[t] = jnp.concatenate([first, positions], axis=0).astype(BF)
        packa[t] = jnp.concatenate([p[0] + k[0], exchanged + k[1]], axis=0).astype(BF)
        packb[t] = jnp.concatenate([p[3] + k[2], swapped + k[3]], axis=0).astype(BF)
        return carry

    lax.fori_loop(0, GROUPS, pack_weights, 0)
    for j in range(QR // 128):
        small[4 * j : 4 * j + 4, :] = q_ref[:, 128 * j : 128 * j + 128].astype(F32)
    qsend[...] = small[...].astype(BF)
    for b in range(HEADS):
        v32[2 * b : 2 * b + 2, :] = vw_ref[...].astype(F32)

    def pack_values(t, carry):
        narrow = pl.multiple_of(t * 512, 128)
        row = iota((8, 128), 0) // 2
        value = jnp.zeros((8, 128), F32)
        for b in range(HEADS):
            value = jnp.where(row == b, v32[:, pl.ds(narrow + b * 128, 128)], value)
        packv[t] = jnp.concatenate([value, jnp.zeros((8, 128), F32)], axis=0).astype(BF)
        return carry

    lax.fori_loop(0, GROUPS, pack_values, 0)

    pl.semaphore_wait(barrier, GROUPS - 1 + 3)

    def scatter(source, target, k, place, arrived, which=range(GROUPS)):
        for i in which:
            s, t = partners[i]
            if i == 0:
                pltpu.make_async_copy(source(slot, me), target.at[place], arrived(0)).start()
            else:
                pltpu.make_async_remote_copy(
                    source(s, t), target.at[place], snd.at[k], arrived(i // BLOCK), here(t), MESH
                ).start()

    def arrive(target, k):
        pltpu.make_async_copy(target, target, rcv.at[k]).wait()

    def q_first(i):
        to = ((zpos + i) % RINGZ) * RINGY + ypos
        return pltpu.make_async_remote_copy(qsend, rq.at[ypos, zpos], qsnd.at[i - 1], qrcv.at[0], here(to), MESH)

    def q_second(i):
        to = zpos * RINGY + (ypos + i) % RINGY
        return pltpu.make_async_remote_copy(
            rq.at[ypos], rq.at[ypos], qsnd.at[RINGZ - 2 + i], qrcv.at[i], here(to), MESH
        )

    scatter(lambda s, t: packa.at[t], rwa, 0, me, lambda c: rcv.at[0])
    pltpu.make_async_copy(qsend, rq.at[ypos, zpos], qrcv.at[0]).start()
    for i in range(1, RINGZ):
        q_first(i).start()
    scatter(lambda s, t: packr.at[t], rwr, 2, me, lambda c: rcv.at[2])

    small[0:8, :] = jnp.zeros((8, 128), F32)
    small[0:4, 0:DR] = nr_ref[...].astype(F32)
    fresh_rope = jnp.concatenate([small[0:8, :], jnp.zeros((120, 128), F32)], axis=0)
    kt[KVR:, CACHE:] = fresh_rope.T.astype(BF)
    kt[KVR + DR :, :CACHE] = jnp.zeros((128 - DR, CACHE), BF)
    for b in range(KVR // 128):
        small[0:8, :] = jnp.zeros((8, 128), F32)
        small[0:4, :] = nl_ref[:, b * 128 : b * 128 + 128].astype(F32)
        fresh = jnp.concatenate([small[0:8, :], jnp.zeros((120, 128), F32)], axis=0)
        latx[CACHE:, b * 128 : b * 128 + 128] = fresh.astype(BF)
    load_lat.wait()
    load_rope.wait()

    def turn(i, carry):
        at = pl.multiple_of(i * 128, 128)
        kt[0:KVR, pl.ds(at, 128)] = latx[pl.ds(at, 128), :].T
        return carry

    lax.fori_loop(0, KEYS // 128, turn, 0)

    def weight_order(blocks):
        o = iota((blocks * 64, 1), 0)
        u = o % 64
        sixth = (u * 43) >> 8
        from_query = sixth * (blocks * 8) + (o // 64) * 8 + (u - sixth * 6)
        from_key = ((u - 48) // 2) * (blocks * 8) + (o // 64) * 8 + 6 + (u % 2)
        return one_hot(jnp.where(u < 48, from_query, from_key), blocks * 64)

    w_order = weight_order(2)
    o = iota((384, 1), 0)
    inside = o % 32
    q_order = one_hot((inside // 4) * 48 + (o // 32) * 4 + inside % 4, 384)
    o = iota((128, 1), 0)
    by_slot = one_hot(((o // 4) % 4) * 32 + (o // 16) * 4 + o % 4, 128)
    by_part = one_hot(((o // 4) % 8) * 16 + (o // 32) * 4 + o % 4, 128)
    halves = one_hot(((o // 8) % 8) * 16 + (o // 64) * 8 + o % 8, 128)
    unhalve = one_hot(((o // 8) % 2) * 64 + (o // 16) * 8 + o % 8, 128)
    sequence = o % 32
    home = ((sequence % 4 + 8 - sequence // 4) % 4) * 8 + sequence // 4
    by_step = one_hot(home * 4 + o // 32, 128)

    def rearranged(order, blocks):
        blocks = [block.reshape(order.shape[1], 128) for block in blocks]
        return mm(order, jnp.concatenate(blocks, axis=1)).astype(BF)

    def eights(ref):
        return [ref[g * BLOCK : (g + 1) * BLOCK] for g in range(NB)]

    def compact(ref, weights, keys=None):
        ordered = rearranged(w_order, eights(ref))
        for b in range(2):
            for g in range(NB):
                lanes = slice(g * 128, g * 128 + 128)
                weights[dp, g * 48 : g * 48 + 48, b * 128 : b * 128 + 128] = ordered[b * 64 : b * 64 + 48, lanes]
                if keys is not None:
                    keys[dp, g * 16 : g * 16 + 16, b * 128 : b * 128 + 128] = ordered[b * 64 + 48 : b * 64 + 64, lanes]

    def ring(pieces, ssem, rsem):
        count = len(pieces)

        def copy(k, p, owner, to, part=None):
            ref = pieces[p]
            rows = ref.shape[1]
            first = 0
            if part is not None:
                rows = rows // 2
                first = part * rows
            view = ref.at[owner, pl.ds(first, rows)]
            at = k * count + p
            return pltpu.make_async_remote_copy(view, view, ssem.at[at], rsem.at[at], {"dp": to, "head": me}, MESH)

        every = range(count)

        def begin():
            for p in every:
                copy(0, p, dp, right, 0).start()
                copy(1, p, dp, left, 1).start()

        def begin_rest():
            for p in every:
                copy(2, p, dp, right, 1).start()
                copy(3, p, dp, left, 0).start()
            for p in every:
                copy(4, p, dp, other).start()

        def forward():
            for p in every:
                copy(0, p, left, right, 0).wait_recv()
                copy(5, p, left, right, 0).start()
                copy(1, p, right, left, 1).wait_recv()
                copy(6, p, right, left, 1).start()

        def neighbours():
            for p in every:
                copy(2, p, left, right, 1).wait_recv()
                copy(7, p, left, other).start()
                copy(3, p, right, left, 0).wait_recv()
                copy(8, p, right, other).start()

        def far():
            for p in every:
                copy(5, p, across, right, 0).wait_recv()
                copy(6, p, across, left, 1).wait_recv()
                copy(9, p, across, other).start()

        def finish():
            sib = 1 - 2 * core
            for p in every:
                copy(4, p, dp + sib, other).wait_recv()
                copy(7, p, left + sib, other).wait_recv()
                copy(8, p, right + sib, other).wait_recv()
                copy(9, p, across + sib, other).wait_recv()

        def close():
            for p in every:
                for k, part in ((0, 0), (1, 1), (2, 1), (3, 0), (4, None), (5, 0), (6, 1), (7, None), (8, None), (9, None)):
                    copy(k, p, dp, right, part).wait_send()

        return begin, begin_rest, forward, neighbours, far, finish, close

    BEGIN, REST, FORWARD, NEIGHBOURS, FAR, FINISH, CLOSE = range(7)
    ring_r = ring([wr], rsnd, rrcv)
    ring_a = ring([wa, ka], xsnd, xrcv)
    ring_b = ring([wb, kb], ysnd, yrcv)
    ring_v = ring([vf], vsnd, vrcv)

    arrive(rwa, 0)
    compact(rwa, wa, ka)
    ring_a[BEGIN]()
    ring_a[REST]()
    eight = rq.at[ypos]
    pltpu.make_async_copy(eight, eight, qrcv.at[0]).wait()
    for i in range(1, RINGY):
        q_second(i).start()
    scatter(lambda s, t: packb.at[t], rwb, 1, me, lambda c: rcv.at[1])
    scatter(lambda s, t: packv.at[t], rv, 3, me, lambda c: rcv.at[3])
    arrive(rwr, 2)
    compact(rwr, wr)
    ring_r[BEGIN]()
    ring_a[FORWARD]()
    ring_r[REST]()
    arrive(rwb, 1)
    compact(rwb, wb, kb)
    ring_b[BEGIN]()
    ring_a[NEIGHBOURS]()
    ring_r[FORWARD]()
    ring_b[REST]()

    for i in range(1, RINGY):
        q_second(i).wait_recv()
    ordered = rearranged(
        q_order,
        [jnp.concatenate([rq[(d + z) % RINGY, z] for z in range(RINGZ)], axis=0) for d in range(RINGY)],
    )
    for j in range(QR // 128):
        for g in range(NB):
            qnat[g * 32 : g * 32 + 32, j * 128 : j * 128 + 128] = ordered[j * 32 : j * 32 + 32, g * 128 : g * 128 + 128]
    ring_a[FAR]()
    ring_a[FINISH]()

    def spread(parts, send, recv, k, sems):
        for c in range(NB):
            d = turns[c]
            rows = [ref[pl.ds(pl.multiple_of(at + d * 32, 32), 32), lanes] for ref, at, lanes in parts]
            block = mm(by_slot, jnp.concatenate(rows, axis=0)).astype(BF)
            send[pl.ds(d * BLOCK, BLOCK)] = block.reshape(BLOCK, 16, block.shape[1])
            scatter(
                lambda s, t: send.at[s], recv, k, slot, lambda c: sems.at[c], range(c * BLOCK, c * BLOCK + BLOCK)
            )

    def absorb(pair, weights, keys, send, recv, k, sems):
        projected = mm(qnat[...], weights[...].reshape(QR, 256))
        plain = (projected[:, 0:128], pltpu.roll(projected[:, 128:256], DR, 1))
        for h in range(2):
            lanes = slice(h * DN, h * DN + DN)
            absq[h * 128 : h * 128 + 128, :] = mm_t(
                plain[h].astype(BF), keys[:, :, lanes].reshape(KVR, DN)
            ).astype(BF)
        parts = [(absq, h * 128, slice(e * 256, e * 256 + 256)) for e in range(2) for h in range(2)]
        spread(parts, send, recv, k, sems)

    absorb(0, wa, ka, senda, recva, 4, arcvd)
    ring_r[NEIGHBOURS]()
    ring_b[FORWARD]()
    ring_r[FAR]()
    ring_r[FINISH]()

    projected = mm(qnat[...], wr[...].reshape(QR, 256))
    posq[:, DR:] = jnp.zeros((ROWS, 128 - DR), BF)
    for h in range(HEADS):
        posq[h * 128 : h * 128 + 128, 0:DR] = projected[:, h * DR : h * DR + DR].astype(BF)
    spread([(posq, h * 128, slice(None)) for h in range(HEADS)], sendr, recvr, 8, rrcvd)
    for step in ring_b[NEIGHBOURS:CLOSE]:
        step()
    absorb(1, wb, kb, sendb, recvb, 5, brcvd)

    o = iota((64, 1), 0)
    v_order = one_hot(((o % 16) // 2) * 16 + (o // 16) * 2 + o % 2, 128)
    arrive(rv, 3)
    ordered = rearranged(v_order, eights(rv))
    for b in range(4):
        for g in range(NB):
            vf[dp, g * 16 : g * 16 + 16, b * 128 : b * 128 + 128] = ordered[b * 16 : b * 16 + 16, g * 128 : g * 128 + 128]
    ring_v[BEGIN]()
    ring_v[REST]()
    ring_v[FORWARD]()

    length = len_ref[0]
    factor = (DN + DR) ** -0.5 * math.log2(math.e)
    chunk = ROWS // 4

    def attend(pair, half, recv, sems):
        classes = [lax.rem(diagonal + NB - c, NB) for c in (2 * half, 2 * half + 1)]
        for e, d in enumerate(classes):
            rows = slice(e * 64, e * 64 + 64)
            mine = pl.ds(d * BLOCK, BLOCK)
            if pair == 0:
                pltpu.make_async_copy(recvr.at[mine], recvr.at[mine], rrcvd.at[2 * half + e]).wait()
                block = mm(halves, recvr[mine].reshape(128, 128)).astype(BF)
                lhs[half, rows, 512:640] = block[0:64]
                lhs[2 + half, rows, 512:640] = block[64:128]
            pltpu.make_async_copy(recv.at[mine], recv.at[mine], sems.at[2 * half + e]).wait()
            block = mm(halves, recv[mine].reshape(128, 256)).astype(BF)
            lhs[2 * pair + half, rows, 0:256] = block[0:64]
            lhs[2 * pair + half, rows, 256:512] = block[64:128]
        scores = mm(lhs[2 * pair + half], kt[...]) * factor
        key = iota((chunk, KEYS), 1)
        step = iota((chunk, 1), 0) % STEPS
        last = jnp.maximum(length - 1, 0)
        keep = (key <= last) | ((key >= CACHE) & (key <= CACHE + step))
        scores = jnp.where(keep, scores, -1e30)
        top = jnp.max(scores, axis=1, keepdims=True)
        raised = jnp.exp2(scores - top)
        total = jnp.sum(raised, axis=1, keepdims=True)
        mixed = (mm(raised.astype(BF), latx[...]) / total).astype(BF)
        for e, d in enumerate(classes):
            stacked = jnp.concatenate(
                [mixed[e * 64 : e * 64 + 64, 0:256], mixed[e * 64 : e * 64 + 64, 256:512]], axis=0
            )
            outs[pair, pl.ds(d * BLOCK, BLOCK)] = mm(unhalve, stacked).astype(BF).reshape(BLOCK, 16, 256)
            turn_back = (NB - 2 * half - e) % NB
            scatter(
                lambda s, t: outs.at[pair, s], back.at[pair], 6 + pair, slot, lambda c: rcv.at[6 + pair],
                range(turn_back * BLOCK, turn_back * BLOCK + BLOCK),
            )

    attend(0, 0, recva, arcvd)
    ring_v[NEIGHBOURS]()
    attend(0, 1, recva, arcvd)
    ring_v[FAR]()
    attend(1, 0, recvb, brcvd)
    attend(1, 1, recvb, brcvd)
    ring_v[FINISH]()

    for pair in range(2):
        arrive(back.at[pair], 6 + pair)
        for d in range(NB):
            block = mm(by_part, back[pair, d * BLOCK : (d + 1) * BLOCK].reshape(128, 256)).astype(BF)
            for e in range(2):
                for h in range(2):
                    at = (e * 2 + h) * 32
                    lt[h, d * 32 : d * 32 + 32, e * 256 : e * 256 + 256] = block[at : at + 32]
        for h in range(2):
            lanes = slice((2 * pair + h) * DV, (2 * pair + h + 1) * DV)
            att[:, lanes] = mm(lt[h], vf[:, :, lanes].reshape(KVR, DV)).astype(BF)
    out_ref[...] = mm(by_step, att[...]).astype(BF).reshape(STEPS, GROUPS, HEADS * DV)

    for k, ref in enumerate((packa, packb, packr, packv, senda, sendb, outs.at[0], outs.at[1], sendr)):
        block = ref.at[pl.ds(0, GROUPS - 1)]
        pltpu.make_async_copy(block, block, snd.at[k]).wait()
    for i in range(1, RINGZ):
        q_first(i).wait_send()
    for i in range(1, RINGY):
        q_second(i).wait_send()
    for steps in (ring_r, ring_a, ring_b, ring_v):
        steps[CLOSE]()


def body(
    query_latent,
    query_weight,
    key_weight,
    value_weight,
    cache_latent,
    cache_rope,
    new_latent,
    new_rope,
    lengths,
):
    vmem = pl.BlockSpec(memory_space=pltpu.VMEM)
    anywhere = pl.BlockSpec(memory_space=pl.ANY)
    smem = pl.BlockSpec(memory_space=pltpu.SMEM)
    dma = pltpu.SemaphoreType.DMA
    return pl.pallas_call(
        kernel,
        out_shape=jax.ShapeDtypeStruct((STEPS, GROUPS, HEADS * DV), BF),
        in_specs=[vmem, vmem, vmem, vmem, anywhere, anywhere, vmem, vmem, smem],
        out_specs=vmem,
        scratch_shapes=[
            pltpu.VMEM((8, GROUPS * 768), F32),
            pltpu.VMEM((8, GROUPS * 512), F32),
            pltpu.VMEM((8, GROUPS * 512), F32),
            pltpu.VMEM((48, 128), F32),
            pltpu.VMEM((GROUPS, 16, 128), BF),
            pltpu.VMEM((GROUPS, 16, 128), BF),
            pltpu.VMEM((GROUPS, 16, 128), BF),
            pltpu.VMEM((GROUPS, 16, 128), BF),
            pltpu.VMEM((48, 128), BF),
            pltpu.VMEM((GROUPS, 16, 128), BF),
            pltpu.VMEM((GROUPS, 16, 128), BF),
            pltpu.VMEM((GROUPS, 16, 128), BF),
            pltpu.VMEM((GROUPS, 16, 128), BF),
            pltpu.VMEM((RINGY, RINGZ, 48, 128), BF),
            pltpu.VMEM((128, QR), BF),
            pltpu.VMEM((DP, 192, 256), BF),
            pltpu.VMEM((DP, 192, 256), BF),
            pltpu.VMEM((DP, 192, 256), BF),
            pltpu.VMEM((DP, 64, 256), BF),
            pltpu.VMEM((DP, 64, 256), BF),
            pltpu.VMEM((DP, 64, 512), BF),
            pltpu.VMEM((ROWS // 2, KVR), BF),
            pltpu.VMEM((ROWS, 128), BF),
            pltpu.VMEM((GROUPS, 16, 128), BF),
            pltpu.VMEM((GROUPS, 16, 256), BF),
            pltpu.VMEM((GROUPS, 16, 256), BF),
            pltpu.VMEM((GROUPS, 16, 128), BF),
            pltpu.VMEM((GROUPS, 16, 256), BF),
            pltpu.VMEM((GROUPS, 16, 256), BF),
            pltpu.VMEM((4, ROWS // 4, WIDE), BF),
            pltpu.VMEM((KEYS, KVR), BF),
            pltpu.VMEM((WIDE, KEYS), BF),
            pltpu.VMEM((2, GROUPS, 16, 256), BF),
            pltpu.VMEM((2, GROUPS, 16, 256), BF),
            pltpu.VMEM((2, 128, KVR), BF),
            pltpu.VMEM((128, HEADS * DV), BF),
            dma((2,)),
            dma((9,)),
            dma((9,)),
            dma((NB,)),
            dma((NB,)),
            dma((NB,)),
            dma((10,)),
            dma((4,)),
            dma((10,)),
            dma((10,)),
            dma((20,)),
            dma((20,)),
            dma((20,)),
            dma((20,)),
            dma((10,)),
            dma((10,)),
        ],
        compiler_params=pltpu.CompilerParams(
            collective_id=0, has_side_effects=True, vmem_limit_bytes=56 * 1024 * 1024
        ),
    )(
        query_latent.reshape(STEPS, QR),
        query_weight,
        key_weight,
        value_weight,
        cache_latent,
        cache_rope,
        new_latent.reshape(STEPS, KVR),
        new_rope.reshape(STEPS, DR),
        lengths,
    )


def solution(mesh):
    placed = (
        P(None, ("dp", "head"), None),
        P(("dp", "head"), None),
        P(("dp", "head"), None),
        P(("dp", "head"), None),
        P(("dp", "head"), None, None),
        P(("dp", "head"), None, None),
        P(None, ("dp", "head"), None),
        P(None, ("dp", "head"), None),
        P(("dp", "head")),
    )
    return jax.shard_map(
        body, mesh=mesh, in_specs=placed, out_specs=P(None, "dp", "head"), check_vma=False
    )
```

```python
import functools
import math

import jax
import jax.numpy as jnp
from jax import lax
from jax.experimental import pallas as pl
from jax.experimental.pallas import tpu as pltpu
from jax.sharding import PartitionSpec as P

QR = 1536
KVR = 512
DN = 128
DR = 64
DV = 128
CACHE = 2048
STEPS = 4
GROUPS = 32
HEADS = 4
RINGX = 4
RINGY = 4
RINGZ = 8
DP = 8
KEYS = CACHE + 128
WIDE = KVR + 128
ROWS = GROUPS * HEADS * STEPS
BLOCK = 8
NB = GROUPS // BLOCK
BF = jnp.bfloat16


def hops(i):
    z, y = i % RINGZ, (i // RINGZ + i) % RINGY
    return min(z, RINGZ - z) + min(y, RINGY - y)


FAR_FIRST = sorted(range(GROUPS), key=lambda i: -hops(i))
F32 = jnp.float32
MESH = pl.DeviceIdType.MESH


def iota(shape, dim):
    return lax.broadcasted_iota(jnp.int32, shape, dim)


def one_hot(source, columns):
    rows = source.shape[0]
    return jnp.where(iota((rows, columns), 1) == source, 1.0, 0.0).astype(BF)


def mm(a, b):
    return jnp.dot(a, b, preferred_element_type=F32)


def mm_t(a, b):
    return lax.dot_general(a, b, (((1,), (1,)), ((), ())), preferred_element_type=F32)


def kernel(
    q_ref, wq_ref, kw_ref, vw_ref, lat_hbm, rope_hbm, nl_ref, nr_ref, len_ref, out_ref,
    w32, k32, v32, small, packr, packa, packb, packv, qsend, rwr, rwa, rwb, rv, rq, qnat, wr, wa, wb, ka, kb, vf,
    absq, posq, sendr, senda, sendb, recvr, recva, recvb, lhs, latx, kt, outs, back, lt, att,
    load_sem, snd, rcv, rrcvd, arcvd, brcvd, qsnd, qrcv, rsnd, rrcv, xsnd, xrcv, ysnd, yrcv, vsnd, vrcv,
):
    dp = lax.axis_index("dp")
    me = lax.axis_index("head")
    xpos = dp // 2
    core = dp % 2
    right = ((xpos + 1) % RINGX) * 2 + core
    left = ((xpos + RINGX - 1) % RINGX) * 2 + core
    across = ((xpos + 2) % RINGX) * 2 + core
    other = xpos * 2 + (1 - core)
    zpos = me // RINGY
    ypos = me % RINGY
    diagonal = (ypos + 2 * RINGY - zpos) % RINGY
    slot = diagonal * RINGZ + zpos

    def here(t):
        return {"dp": dp, "head": t}

    turns = [lax.rem(diagonal + k, RINGY) for k in range(RINGY)]
    planes = [lax.rem(zpos + i, RINGZ) for i in range(RINGZ)]
    partners = [(d * RINGZ + z, z * RINGY + lax.rem(d + z, RINGY)) for d in turns for z in planes]

    barrier = pltpu.get_barrier_semaphore()

    for _, t in [partners[i] for i in FAR_FIRST if i > 0]:
        pl.semaphore_signal(barrier, inc=1, device_id=here(t), device_id_type=MESH)
    for d in (left, right, other):
        pl.semaphore_signal(barrier, inc=1, device_id={"dp": d, "head": me}, device_id_type=MESH)

    load_lat = pltpu.make_async_copy(lat_hbm.at[0], latx.at[pl.ds(0, CACHE)], load_sem.at[0])
    load_rope = pltpu.make_async_copy(rope_hbm.at[0], kt.at[pl.ds(KVR, DR), pl.ds(0, CACHE)], load_sem.at[1])
    load_lat.start()
    load_rope.start()

    w32[6:8, :] = jnp.zeros((2, w32.shape[1]), F32)
    w32[0:6, :] = wq_ref[...].astype(F32)
    k32[0:6, :] = jnp.zeros((6, k32.shape[1]), F32)
    k32[6:8, :] = kw_ref[...].astype(F32)

    def pack_weights(t, carry):
        wide = pl.multiple_of(t * 768, 128)
        narrow = pl.multiple_of(t * 512, 128)
        p = [w32[:, pl.ds(wide + b * 128, 128)] for b in range(6)]
        k = [k32[:, pl.ds(narrow + b * 128, 128)] for b in range(4)]
        low = iota((8, 128), 1) < DR
        positions = jnp.where(low, p[4], p[5])
        swapped = jnp.where(low, p[5], p[4])
        first = jnp.where(low, p[1], p[2])
        exchanged = jnp.where(low, p[2], p[1])
        packr[t] = jnp.concatenate([first, positions], axis=0).astype(BF)
        packa[t] = jnp.concatenate([p[0] + k[0], exchanged + k[1]], axis=0).astype(BF)
        packb[t] = jnp.concatenate([p[3] + k[2], swapped + k[3]], axis=0).astype(BF)
        return carry

    lax.fori_loop(0, GROUPS, pack_weights, 0)
    for j in range(QR // 128):
        small[4 * j : 4 * j + 4, :] = q_ref[:, 128 * j : 128 * j + 128].astype(F32)
    qsend[...] = small[...].astype(BF)
    for b in range(HEADS):
        v32[2 * b : 2 * b + 2, :] = vw_ref[...].astype(F32)

    def pack_values(t, carry):
        narrow = pl.multiple_of(t * 512, 128)
        row = iota((8, 128), 0) // 2
        value = jnp.zeros((8, 128), F32)
        for b in range(HEADS):
            value = jnp.where(row == b, v32[:, pl.ds(narrow + b * 128, 128)], value)
        packv[t] = jnp.concatenate([value, jnp.zeros((8, 128), F32)], axis=0).astype(BF)
        return carry

    lax.fori_loop(0, GROUPS, pack_values, 0)

    pl.semaphore_wait(barrier, GROUPS - 1 + 3)

    def scatter(source, target, k, place, arrived, which=FAR_FIRST):
        for i in sorted(which, key=lambda i: -hops(i)):
            s, t = partners[i]
            if i == 0:
                pltpu.make_async_copy(source(slot, me), target.at[place], arrived(0)).start()
            else:
                pltpu.make_async_remote_copy(
                    source(s, t), target.at[place], snd.at[k], arrived(i // BLOCK), here(t), MESH
                ).start()

    def arrive(target, k):
        pltpu.make_async_copy(target, target, rcv.at[k]).wait()

    def q_first(i):
        to = ((zpos + i) % RINGZ) * RINGY + ypos
        return pltpu.make_async_remote_copy(qsend, rq.at[ypos, zpos], qsnd.at[i - 1], qrcv.at[0], here(to), MESH)

    def q_second(i):
        to = zpos * RINGY + (ypos + i) % RINGY
        return pltpu.make_async_remote_copy(
            rq.at[ypos], rq.at[ypos], qsnd.at[RINGZ - 2 + i], qrcv.at[i], here(to), MESH
        )

    scatter(lambda s, t: packa.at[t], rwa, 0, me, lambda c: rcv.at[0])
    pltpu.make_async_copy(qsend, rq.at[ypos, zpos], qrcv.at[0]).start()
    for i in (4, 3, 5, 2, 6, 1, 7):
        q_first(i).start()
    scatter(lambda s, t: packr.at[t], rwr, 2, me, lambda c: rcv.at[2])

    small[0:8, :] = jnp.zeros((8, 128), F32)
    small[0:4, 0:DR] = nr_ref[...].astype(F32)
    fresh_rope = jnp.concatenate([small[0:8, :], jnp.zeros((120, 128), F32)], axis=0)
    kt[KVR:, CACHE:] = fresh_rope.T.astype(BF)
    kt[KVR + DR :, :CACHE] = jnp.zeros((128 - DR, CACHE), BF)
    for b in range(KVR // 128):
        small[0:8, :] = jnp.zeros((8, 128), F32)
        small[0:4, :] = nl_ref[:, b * 128 : b * 128 + 128].astype(F32)
        fresh = jnp.concatenate([small[0:8, :], jnp.zeros((120, 128), F32)], axis=0)
        latx[CACHE:, b * 128 : b * 128 + 128] = fresh.astype(BF)
    load_lat.wait()
    load_rope.wait()

    def turn(i, carry):
        at = pl.multiple_of(i * 128, 128)
        kt[0:KVR, pl.ds(at, 128)] = latx[pl.ds(at, 128), :].T
        return carry

    lax.fori_loop(0, KEYS // 128, turn, 0)

    def weight_order(blocks):
        o = iota((blocks * 64, 1), 0)
        u = o % 64
        sixth = (u * 43) >> 8
        from_query = sixth * (blocks * 8) + (o // 64) * 8 + (u - sixth * 6)
        from_key = ((u - 48) // 2) * (blocks * 8) + (o // 64) * 8 + 6 + (u % 2)
        return one_hot(jnp.where(u < 48, from_query, from_key), blocks * 64)

    w_order = weight_order(2)
    o = iota((384, 1), 0)
    inside = o % 32
    q_order = one_hot((inside // 4) * 48 + (o // 32) * 4 + inside % 4, 384)
    o = iota((128, 1), 0)
    by_slot = one_hot(((o // 4) % 4) * 32 + (o // 16) * 4 + o % 4, 128)
    by_part = one_hot(((o // 4) % 8) * 16 + (o // 32) * 4 + o % 4, 128)
    halves = one_hot(((o // 8) % 8) * 16 + (o // 64) * 8 + o % 8, 128)
    unhalve = one_hot(((o // 8) % 2) * 64 + (o // 16) * 8 + o % 8, 128)
    sequence = o % 32
    home = ((sequence % 4 + 8 - sequence // 4) % 4) * 8 + sequence // 4
    by_step = one_hot(home * 4 + o // 32, 128)

    def rearranged(order, blocks):
        blocks = [block.reshape(order.shape[1], 128) for block in blocks]
        return mm(order, jnp.concatenate(blocks, axis=1)).astype(BF)

    def eights(ref):
        return [ref[g * BLOCK : (g + 1) * BLOCK] for g in range(NB)]

    def compact(ref, weights, keys=None):
        ordered = rearranged(w_order, eights(ref))
        for b in range(2):
            for g in range(NB):
                lanes = slice(g * 128, g * 128 + 128)
                weights[dp, g * 48 : g * 48 + 48, b * 128 : b * 128 + 128] = ordered[b * 64 : b * 64 + 48, lanes]
                if keys is not None:
                    keys[dp, g * 16 : g * 16 + 16, b * 128 : b * 128 + 128] = ordered[b * 64 + 48 : b * 64 + 64, lanes]

    def ring(pieces, ssem, rsem):
        count = len(pieces)

        def copy(k, p, owner, to, part=None):
            ref = pieces[p]
            rows = ref.shape[1]
            first = 0
            if part is not None:
                rows = rows // 2
                first = part * rows
            view = ref.at[owner, pl.ds(first, rows)]
            at = k * count + p
            return pltpu.make_async_remote_copy(view, view, ssem.at[at], rsem.at[at], {"dp": to, "head": me}, MESH)

        every = range(count)

        def begin():
            for p in every:
                copy(0, p, dp, right, 0).start()
                copy(1, p, dp, left, 1).start()

        def begin_rest():
            for p in every:
                copy(2, p, dp, right, 1).start()
                copy(3, p, dp, left, 0).start()
            for p in every:
                copy(4, p, dp, other).start()

        def forward():
            for p in every:
                copy(0, p, left, right, 0).wait_recv()
                copy(5, p, left, right, 0).start()
                copy(1, p, right, left, 1).wait_recv()
                copy(6, p, right, left, 1).start()

        def neighbours():
            for p in every:
                copy(2, p, left, right, 1).wait_recv()
                copy(7, p, left, other).start()
                copy(3, p, right, left, 0).wait_recv()
                copy(8, p, right, other).start()

        def far():
            for p in every:
                copy(5, p, across, right, 0).wait_recv()
                copy(6, p, across, left, 1).wait_recv()
                copy(9, p, across, other).start()

        def finish():
            sib = 1 - 2 * core
            for p in every:
                copy(4, p, dp + sib, other).wait_recv()
                copy(7, p, left + sib, other).wait_recv()
                copy(8, p, right + sib, other).wait_recv()
                copy(9, p, across + sib, other).wait_recv()

        def close():
            for p in every:
                for k, part in ((0, 0), (1, 1), (2, 1), (3, 0), (4, None), (5, 0), (6, 1), (7, None), (8, None), (9, None)):
                    copy(k, p, dp, right, part).wait_send()

        return begin, begin_rest, forward, neighbours, far, finish, close

    BEGIN, REST, FORWARD, NEIGHBOURS, FAR, FINISH, CLOSE = range(7)
    ring_r = ring([wr], rsnd, rrcv)
    ring_a = ring([wa, ka], xsnd, xrcv)
    ring_b = ring([wb, kb], ysnd, yrcv)
    ring_v = ring([vf], vsnd, vrcv)

    arrive(rwa, 0)
    compact(rwa, wa, ka)
    ring_a[BEGIN]()
    ring_a[REST]()
    eight = rq.at[ypos]
    pltpu.make_async_copy(eight, eight, qrcv.at[0]).wait()
    for i in range(1, RINGY):
        q_second(i).start()
    scatter(lambda s, t: packb.at[t], rwb, 1, me, lambda c: rcv.at[1])
    scatter(lambda s, t: packv.at[t], rv, 3, me, lambda c: rcv.at[3])
    arrive(rwr, 2)
    compact(rwr, wr)
    ring_r[BEGIN]()
    ring_a[FORWARD]()
    ring_r[REST]()
    ring_r[FORWARD]()
    ring_a[NEIGHBOURS]()
    ring_a[FAR]()
    arrive(rwb, 1)
    compact(rwb, wb, kb)
    ring_b[BEGIN]()
    ring_b[REST]()
    for i in range(1, RINGY):
        q_second(i).wait_recv()
    ordered = rearranged(
        q_order,
        [jnp.concatenate([rq[(d + z) % RINGY, z] for z in range(RINGZ)], axis=0) for d in range(RINGY)],
    )
    for j in range(QR // 128):
        for g in range(NB):
            qnat[g * 32 : g * 32 + 32, j * 128 : j * 128 + 128] = ordered[j * 32 : j * 32 + 32, g * 128 : g * 128 + 128]
    ring_a[FINISH]()
    ring_r[NEIGHBOURS]()

    def spread(parts, send, recv, k, sems):
        for c in range(NB):
            d = turns[c]
            rows = [ref[pl.ds(pl.multiple_of(at + d * 32, 32), 32), lanes] for ref, at, lanes in parts]
            block = mm(by_slot, jnp.concatenate(rows, axis=0)).astype(BF)
            send[pl.ds(d * BLOCK, BLOCK)] = block.reshape(BLOCK, 16, block.shape[1])
            scatter(
                lambda s, t: send.at[s], recv, k, slot, lambda c: sems.at[c], range(c * BLOCK, c * BLOCK + BLOCK)
            )

    def absorb(pair, weights, keys, send, recv, k, sems):
        projected = mm(qnat[...], weights[...].reshape(QR, 256))
        plain = (projected[:, 0:128], pltpu.roll(projected[:, 128:256], DR, 1))
        for h in range(2):
            lanes = slice(h * DN, h * DN + DN)
            absq[h * 128 : h * 128 + 128, :] = mm_t(
                plain[h].astype(BF), keys[:, :, lanes].reshape(KVR, DN)
            ).astype(BF)
        parts = [(absq, h * 128, slice(e * 256, e * 256 + 256)) for e in range(2) for h in range(2)]
        spread(parts, send, recv, k, sems)

    absorb(0, wa, ka, senda, recva, 4, arcvd)
    ring_r[FAR]()
    ring_b[FORWARD]()
    ring_r[FINISH]()

    projected = mm(qnat[...], wr[...].reshape(QR, 256))
    posq[:, DR:] = jnp.zeros((ROWS, 128 - DR), BF)
    for h in range(HEADS):
        posq[h * 128 : h * 128 + 128, 0:DR] = projected[:, h * DR : h * DR + DR].astype(BF)
    spread([(posq, h * 128, slice(None)) for h in range(HEADS)], sendr, recvr, 8, rrcvd)
    ring_b[NEIGHBOURS]()
    ring_b[FAR]()
    ring_b[FINISH]()
    absorb(1, wb, kb, sendb, recvb, 5, brcvd)

    o = iota((64, 1), 0)
    v_order = one_hot(((o % 16) // 2) * 16 + (o // 16) * 2 + o % 2, 128)
    arrive(rv, 3)
    ordered = rearranged(v_order, eights(rv))
    for b in range(4):
        for g in range(NB):
            vf[dp, g * 16 : g * 16 + 16, b * 128 : b * 128 + 128] = ordered[b * 16 : b * 16 + 16, g * 128 : g * 128 + 128]
    ring_v[BEGIN]()
    ring_v[REST]()
    ring_v[FORWARD]()

    length = len_ref[0]
    factor = (DN + DR) ** -0.5 * math.log2(math.e)
    chunk = ROWS // 4

    def attend(pair, half, recv, sems):
        classes = [lax.rem(diagonal + NB - c, NB) for c in (2 * half, 2 * half + 1)]
        for e, d in enumerate(classes):
            rows = slice(e * 64, e * 64 + 64)
            mine = pl.ds(d * BLOCK, BLOCK)
            if pair == 0:
                pltpu.make_async_copy(recvr.at[mine], recvr.at[mine], rrcvd.at[2 * half + e]).wait()
                block = mm(halves, recvr[mine].reshape(128, 128)).astype(BF)
                lhs[half, rows, 512:640] = block[0:64]
                lhs[2 + half, rows, 512:640] = block[64:128]
            pltpu.make_async_copy(recv.at[mine], recv.at[mine], sems.at[2 * half + e]).wait()
            block = mm(halves, recv[mine].reshape(128, 256)).astype(BF)
            lhs[2 * pair + half, rows, 0:256] = block[0:64]
            lhs[2 * pair + half, rows, 256:512] = block[64:128]
        scores = mm(lhs[2 * pair + half], kt[...]) * factor
        key = iota((chunk, KEYS), 1)
        step = iota((chunk, 1), 0) % STEPS
        last = jnp.maximum(length - 1, 0)
        keep = (key <= last) | ((key >= CACHE) & (key <= CACHE + step))
        scores = jnp.where(keep, scores, -1e30)
        top = jnp.max(scores, axis=1, keepdims=True)
        raised = jnp.exp2(scores - top)
        total = jnp.sum(raised, axis=1, keepdims=True)
        mixed = (mm(raised.astype(BF), latx[...]) / total).astype(BF)
        for e, d in enumerate(classes):
            stacked = jnp.concatenate(
                [mixed[e * 64 : e * 64 + 64, 0:256], mixed[e * 64 : e * 64 + 64, 256:512]], axis=0
            )
            outs[pair, pl.ds(d * BLOCK, BLOCK)] = mm(unhalve, stacked).astype(BF).reshape(BLOCK, 16, 256)
            turn_back = (NB - 2 * half - e) % NB
            scatter(
                lambda s, t: outs.at[pair, s], back.at[pair], 6 + pair, slot, lambda c: rcv.at[6 + pair],
                range(turn_back * BLOCK, turn_back * BLOCK + BLOCK),
            )

    attend(0, 0, recva, arcvd)
    ring_v[NEIGHBOURS]()
    attend(0, 1, recva, arcvd)
    ring_v[FAR]()
    attend(1, 0, recvb, brcvd)
    attend(1, 1, recvb, brcvd)
    ring_v[FINISH]()

    for pair in range(2):
        arrive(back.at[pair], 6 + pair)
        for d in range(NB):
            block = mm(by_part, back[pair, d * BLOCK : (d + 1) * BLOCK].reshape(128, 256)).astype(BF)
            for e in range(2):
                for h in range(2):
                    at = (e * 2 + h) * 32
                    lt[h, d * 32 : d * 32 + 32, e * 256 : e * 256 + 256] = block[at : at + 32]
        for h in range(2):
            lanes = slice((2 * pair + h) * DV, (2 * pair + h + 1) * DV)
            att[:, lanes] = mm(lt[h], vf[:, :, lanes].reshape(KVR, DV)).astype(BF)
    out_ref[...] = mm(by_step, att[...]).astype(BF).reshape(STEPS, GROUPS, HEADS * DV)

    for k, ref in enumerate((packa, packb, packr, packv, senda, sendb, outs.at[0], outs.at[1], sendr)):
        block = ref.at[pl.ds(0, GROUPS - 1)]
        pltpu.make_async_copy(block, block, snd.at[k]).wait()
    for i in range(1, RINGZ):
        q_first(i).wait_send()
    for i in range(1, RINGY):
        q_second(i).wait_send()
    for steps in (ring_r, ring_a, ring_b, ring_v):
        steps[CLOSE]()


def body(
    query_latent,
    query_weight,
    key_weight,
    value_weight,
    cache_latent,
    cache_rope,
    new_latent,
    new_rope,
    lengths,
):
    vmem = pl.BlockSpec(memory_space=pltpu.VMEM)
    anywhere = pl.BlockSpec(memory_space=pl.ANY)
    smem = pl.BlockSpec(memory_space=pltpu.SMEM)
    dma = pltpu.SemaphoreType.DMA
    return pl.pallas_call(
        kernel,
        out_shape=jax.ShapeDtypeStruct((STEPS, GROUPS, HEADS * DV), BF),
        in_specs=[vmem, vmem, vmem, vmem, anywhere, anywhere, vmem, vmem, smem],
        out_specs=vmem,
        scratch_shapes=[
            pltpu.VMEM((8, GROUPS * 768), F32),
            pltpu.VMEM((8, GROUPS * 512), F32),
            pltpu.VMEM((8, GROUPS * 512), F32),
            pltpu.VMEM((48, 128), F32),
            pltpu.VMEM((GROUPS, 16, 128), BF),
            pltpu.VMEM((GROUPS, 16, 128), BF),
            pltpu.VMEM((GROUPS, 16, 128), BF),
            pltpu.VMEM((GROUPS, 16, 128), BF),
            pltpu.VMEM((48, 128), BF),
            pltpu.VMEM((GROUPS, 16, 128), BF),
            pltpu.VMEM((GROUPS, 16, 128), BF),
            pltpu.VMEM((GROUPS, 16, 128), BF),
            pltpu.VMEM((GROUPS, 16, 128), BF),
            pltpu.VMEM((RINGY, RINGZ, 48, 128), BF),
            pltpu.VMEM((128, QR), BF),
            pltpu.VMEM((DP, 192, 256), BF),
            pltpu.VMEM((DP, 192, 256), BF),
            pltpu.VMEM((DP, 192, 256), BF),
            pltpu.VMEM((DP, 64, 256), BF),
            pltpu.VMEM((DP, 64, 256), BF),
            pltpu.VMEM((DP, 64, 512), BF),
            pltpu.VMEM((ROWS // 2, KVR), BF),
            pltpu.VMEM((ROWS, 128), BF),
            pltpu.VMEM((GROUPS, 16, 128), BF),
            pltpu.VMEM((GROUPS, 16, 256), BF),
            pltpu.VMEM((GROUPS, 16, 256), BF),
            pltpu.VMEM((GROUPS, 16, 128), BF),
            pltpu.VMEM((GROUPS, 16, 256), BF),
            pltpu.VMEM((GROUPS, 16, 256), BF),
            pltpu.VMEM((4, ROWS // 4, WIDE), BF),
            pltpu.VMEM((KEYS, KVR), BF),
            pltpu.VMEM((WIDE, KEYS), BF),
            pltpu.VMEM((2, GROUPS, 16, 256), BF),
            pltpu.VMEM((2, GROUPS, 16, 256), BF),
            pltpu.VMEM((2, 128, KVR), BF),
            pltpu.VMEM((128, HEADS * DV), BF),
            dma((2,)),
            dma((9,)),
            dma((9,)),
            dma((NB,)),
            dma((NB,)),
            dma((NB,)),
            dma((10,)),
            dma((4,)),
            dma((10,)),
            dma((10,)),
            dma((20,)),
            dma((20,)),
            dma((20,)),
            dma((20,)),
            dma((10,)),
            dma((10,)),
        ],
        compiler_params=pltpu.CompilerParams(
            collective_id=0, has_side_effects=True, vmem_limit_bytes=56 * 1024 * 1024
        ),
    )(
        query_latent.reshape(STEPS, QR),
        query_weight,
        key_weight,
        value_weight,
        cache_latent,
        cache_rope,
        new_latent.reshape(STEPS, KVR),
        new_rope.reshape(STEPS, DR),
        lengths,
    )


def solution(mesh):
    placed = (
        P(None, ("dp", "head"), None),
        P(("dp", "head"), None),
        P(("dp", "head"), None),
        P(("dp", "head"), None),
        P(("dp", "head"), None, None),
        P(("dp", "head"), None, None),
        P(None, ("dp", "head"), None),
        P(None, ("dp", "head"), None),
        P(("dp", "head")),
    )
    return jax.shard_map(
        body, mesh=mesh, in_specs=placed, out_specs=P(None, "dp", "head"), check_vma=False
    )
```
